32 devices in a mesh: ctx: 4 (over y, x), ch: 8 (over z, core).
Axes of the slice: x: 2, y: 2, z: 4, core: 2. Of those that a mesh axis runs over, the one named last changes fastest.
Arguments:
- queries: bfloat16 [4096, 4096], P('ctx', 'ch'), may hold values from -12 to 12
- key_input: bfloat16 [4096, 4096], P('ctx', 'ch'), may hold values from -6 to 6
- value_input: bfloat16 [4096, 4096], P('ctx', 'ch'), may hold values from -6 to 6
- filters: bfloat16 [4096, 4096], P('ctx', 'ch'), may hold values from -0.3 to 0.3
- skip_gain: float32 [4096], P('ch'), may hold values from -0.3 to 0.3
- out_weight: bfloat16 [4096, 4096], P('ch'), may hold values from -0.125 to 0.125
Outputs:
- layer_out: bfloat16 [4096, 4096], P('ctx', 'ch')
The draws below stay inside these ranges and needn't reach their ends.
All inputs are finite; a program needn't handle non-finite values.
Results may differ from the reference program's by a relative error of at most 0.019.
Values may be sent and summed in bfloat16 or wider, within the bound.
A program may use at most 320 MiB of HBM per device.

```python
import math
import jax
import jax.numpy as jnp
from jax import lax

D = 4096
TOKENS = 4096
N_CH = 8


def draw_filters(key, part):
    key_pick, key_slow, key_fast, key_head, key_tail, key_weight = jax.random.split(key, 6)
    positions = jnp.arange(TOKENS, dtype=jnp.float32)[:, None]
    slow_rate = jnp.exp(jax.random.uniform(key_slow, (D,), jnp.float32, jnp.log(0.1), jnp.log(1.0))) / TOKENS
    fast_rate = jnp.exp(jax.random.uniform(key_fast, (D,), jnp.float32, jnp.log(1.0 / 60.0), jnp.log(1.0 / 30.0)))
    head_weight = jax.random.uniform(key_weight, (D,), jnp.float32, 0.15, 0.35)
    chosen = jax.random.bernoulli(key_pick, 0.5, (D,))
    head_scale = jnp.where(chosen, head_weight * jnp.sqrt(2.0 * fast_rate), 0.0)
    head_env = head_scale[None, :] * jnp.exp(-fast_rate[None, :] * positions)
    tail_env = 0.13 / math.sqrt(TOKENS) * jnp.exp(-slow_rate[None, :] * positions)
    head_noise = jax.random.truncated_normal(key_head, -3.0, 3.0, (TOKENS, D), jnp.float32)
    tail_noise = jax.random.truncated_normal(key_tail, -3.0, 3.0, (TOKENS, D), jnp.float32)
    return (head_env * head_noise + tail_env * tail_noise).astype(jnp.bfloat16)


def strengthened(result, stream_key, source, target, shards_of, factor):
    def block_of(axis_at):
        return (jnp.arange(result.shape[axis_at]) // (result.shape[axis_at] // shards_of)).reshape((-1,) + (1,) * (result.ndim - 1 - axis_at))

    first = jax.random.permutation(stream_key, shards_of)[block_of(target)]
    far = (block_of(target) + shards_of // 2) % shards_of
    return jnp.where((block_of(source) == first) | (block_of(source) == far), factor * result, result)


def block_levels(rng, shape, cuts, least, largest):
    def one(axis_at, parts):
        steps = jax.random.uniform(jax.random.fold_in(jax.random.fold_in(rng, 6), axis_at), (parts,), jnp.float32, least / len(cuts), largest / len(cuts))
        return jnp.repeat(jnp.exp(steps), shape[axis_at] // parts).reshape((-1,) + (1,) * (len(shape) - axis_at - 1))

    gain = one(*cuts[0])
    for cut in cuts[1:]:
        gain = gain * one(*cut)
    return gain


def scatter_about(own_key, extent, deviation, bound, pieces=(), held_as=jnp.bfloat16):
    array = jax.random.normal(own_key, extent, jnp.float32) * deviation
    if len(pieces) > 0:
        array = block_levels(own_key, extent, pieces, -0.22, 0.18) * array
    return jnp.clip(array, min=-bound, max=bound).astype(held_as)


def noise_with(stream_key, dims, scale, reach, pieces, heavy, held_as=jnp.bfloat16):
    entries = scale * jax.random.normal(stream_key, dims, jnp.float32)
    if pieces:
        entries = entries * block_levels(stream_key, dims, pieces, -0.22, 0.18)
    return jnp.clip(strengthened(entries, jax.random.fold_in(stream_key, 3), *heavy), -reach, reach).astype(held_as)


def setup_inputs(seed: int = 0) -> dict:
    streams_of = jax.random.split(jax.random.key(seed), 7)
    return {
        "queries": scatter_about(streams_of[0], (TOKENS, D), 2.0, 12.0, ((0, 4), (1, 8))),
        "key_input": scatter_about(streams_of[1], (TOKENS, D), 1.0, 6.0, ((0, 4), (1, 8))),
        "value_input": scatter_about(streams_of[2], (TOKENS, D), 1.0, 6.0, ((0, 4), (1, 8))),
        "filters": draw_filters(jax.random.fold_in(streams_of[6], 71), 0),
        "skip_gain": jnp.clip(jax.random.uniform(streams_of[4], (D,), jnp.float32, -0.3, 0.3) * block_levels(streams_of[4], (D,), ((0, 8),), -0.4, 0.0), -0.3, 0.3),
        "out_weight": noise_with(streams_of[5], (D, D), D ** -0.5, 0.125, ((0, 8),), (0, 1, 8, 2.0)),
    }


def reference(queries, key_input, value_input, filters, skip_gain, out_weight):
    mixed_in = (key_input.astype(jnp.float32) * value_input.astype(jnp.float32)).astype(jnp.bfloat16)
    width = D // N_CH
    groups = D // width
    length = 2 * TOKENS

    def convolve(pair):
        signal, kernel = pair
        product = jnp.fft.rfft(signal, n=length, axis=0) * jnp.fft.rfft(kernel, n=length, axis=0)
        return jnp.fft.irfft(product, n=length, axis=0)[:TOKENS]

    signals = mixed_in.astype(jnp.float32).reshape(TOKENS, groups, width).transpose(1, 0, 2)
    kernels = filters.astype(jnp.float32).reshape(TOKENS, groups, width).transpose(1, 0, 2)
    conv = lax.map(convolve, (signals, kernels))
    conv = conv.transpose(1, 0, 2).reshape(TOKENS, D)
    gated = (queries.astype(jnp.float32) * (conv + skip_gain[None, :] * mixed_in.astype(jnp.float32))).astype(jnp.bfloat16)
    gated_parts = gated.reshape(TOKENS, groups, width).transpose(1, 0, 2)
    weight_parts = out_weight.reshape(groups, width, D)

    def accumulate(total, pair):
        part_rows, part_weight = pair
        term = jnp.dot(part_rows, part_weight, preferred_element_type=jnp.float32).astype(jnp.bfloat16)
        term = lax.optimization_barrier(term)
        return total + term.astype(jnp.float32), None

    total, unused = lax.scan(accumulate, jnp.zeros((TOKENS, D), jnp.float32), (gated_parts, weight_parts))
    return total.astype(jnp.bfloat16)
```

```python
import functools
import math

import jax
import jax.numpy as jnp
import numpy as np
from jax import lax
from jax.experimental import pallas as pl
from jax.experimental.pallas import tpu as pltpu
from jax.sharding import PartitionSpec as P

BLOCK = 256
F32 = jnp.float32
BF16 = jnp.bfloat16


def transform_tables(block):
    k = np.arange(block)[:, None]
    n = np.arange(block)[None, :]
    angle = np.pi * (((2 * k + 1) * n) % (4 * block)) / (2 * block)
    forward = np.concatenate([np.cos(angle), -np.sin(angle)], axis=0)
    backward = np.concatenate([np.cos(angle).T, -np.sin(angle).T], axis=1) / block

    def halves(table):
        high = table.astype(BF16)
        low = (table - high.astype(np.float64)).astype(BF16)
        return high, low

    f_high, f_low = halves(forward)
    b_high, b_low = halves(backward)
    return np.stack([f_high, f_low]), np.stack([b_high, b_low])


def dot(left, right):
    return jnp.dot(left, right, preferred_element_type=F32)


def conv_kernel(pair_ref, f_ref, b_ref, out_ref, spec, prod):
    nb, block, width2 = pair_ref.shape
    width = width2 // 2

    def ahead(p, carry):
        data = pair_ref[p]
        spec[p] = dot(f_ref[0], data) + dot(f_ref[1], data)
        return carry

    lax.fori_loop(0, nb, ahead, 0)

    rows = 8
    sign = 1.0 - 2.0 * (lax.broadcasted_iota(jnp.int32, (rows, width), 0) % 2).astype(F32)

    def products(chunk, carry):
        top = pl.multiple_of(chunk * rows, rows)
        re = pl.ds(top, rows)
        im = pl.ds(pl.multiple_of(block + top, rows), rows)
        x = [(spec[p, re, :width], spec[p, im, :width]) for p in range(nb)]
        h = [(spec[p, re, width:], spec[p, im, width:]) for p in range(nb)]
        last = None
        for j in range(nb):
            zr = zi = None
            for p in range(j + 1):
                xr, xi = x[p]
                hr, hi = h[j - p]
                tr = xr * hr - xi * hi
                ti = xr * hi + xi * hr
                zr = tr if zr is None else zr + tr
                zi = ti if zi is None else zi + ti
            if last is None:
                yr, yi = zr, zi
            else:
                yr = zr - sign * last[1]
                yi = zi + sign * last[0]
            last = (zr, zi)
            prod[j, re, :] = yr
            prod[j, im, :] = yi
        return carry

    lax.fori_loop(0, block // rows, products, 0)

    def back(j, carry):
        data = jnp.concatenate([prod[2 * j], prod[2 * j + 1]], axis=1)
        high = data.astype(BF16)
        low = (data - high.astype(F32)).astype(BF16)
        conv = (dot(b_ref[0], high) + (dot(b_ref[0], low) + dot(b_ref[1], high))).astype(BF16)
        out_ref[2 * j] = conv[:, :width]
        out_ref[2 * j + 1] = conv[:, width:]
        return carry

    lax.fori_loop(0, nb // 2, back, 0)


def causal_conv(pair):
    total, width2 = pair.shape
    width = width2 // 2
    nb = total // BLOCK
    forward, backward = transform_tables(BLOCK)
    out = pl.pallas_call(
        conv_kernel,
        out_shape=jax.ShapeDtypeStruct((nb, BLOCK, width), BF16),
        in_specs=[pl.BlockSpec(memory_space=pltpu.VMEM)] * 3,
        out_specs=pl.BlockSpec(memory_space=pltpu.VMEM),
        scratch_shapes=[
            pltpu.VMEM((nb, 2 * BLOCK, width2), F32),
            pltpu.VMEM((nb, 2 * BLOCK, width), F32),
        ],
        compiler_params=pltpu.CompilerParams(vmem_limit_bytes=48 * 1024 * 1024),
        cost_estimate=pl.CostEstimate(
            flops=14 * total * BLOCK * width2, bytes_accessed=6 * total * width, transcendentals=0
        ),
    )(pair.reshape(nb, BLOCK, width2), jnp.asarray(forward), jnp.asarray(backward))
    return out.reshape(total, width)


def per_device(queries, key_input, value_input, filters, skip_gain, out_weight):
    tok_rows, channels = queries.shape
    n_ctx = lax.axis_size("ctx")
    width = channels // n_ctx
    mixed_in = (key_input.astype(F32) * value_input.astype(F32)).astype(BF16)
    split = lambda a: a.reshape(tok_rows, n_ctx, width)
    pair = jnp.concatenate([split(mixed_in), split(filters)], axis=2).transpose(1, 0, 2)
    pair = lax.all_to_all(pair, "ctx", 0, 0, tiled=True)
    conv = causal_conv(pair.reshape(n_ctx * tok_rows, 2 * width))
    conv = lax.all_to_all(conv.reshape(n_ctx, tok_rows, width), "ctx", 0, 0, tiled=True)
    conv = conv.transpose(1, 0, 2).reshape(tok_rows, channels).astype(F32)
    gated = (
        queries.astype(F32) * (conv + skip_gain[None, :] * mixed_in.astype(F32))
    ).astype(BF16)
    shares = lax.psum_scatter(
        lax.dot_general(
            out_weight, gated, (((0,), (1,)), ((), ())), preferred_element_type=F32
        ).astype(BF16),
        "ch",
        scatter_dimension=0,
        tiled=True,
    ).astype(F32)
    return shares.T.astype(BF16)


def solution(mesh):
    in_specs = (
        P("ctx", "ch"),
        P("ctx", "ch"),
        P("ctx", "ch"),
        P("ctx", "ch"),
        P("ch"),
        P("ch", None),
    )
    return jax.shard_map(
        per_device, mesh=mesh, in_specs=in_specs, out_specs=P("ctx", "ch"), check_vma=False
    )
```

```python
import functools

import jax
import jax.numpy as jnp
import numpy as np
from jax import lax
from jax.experimental import pallas as pl
from jax.experimental.pallas import tpu as pltpu
from jax.sharding import PartitionSpec as P

BLOCK = 256
F32 = jnp.float32
BF16 = jnp.bfloat16


def transform_tables(block):
    k = np.arange(block)[:, None]
    n = np.arange(block)[None, :]
    angle = np.pi * (((2 * k + 1) * n) % (4 * block)) / (2 * block)
    forward = np.concatenate([np.cos(angle), -np.sin(angle)], axis=0)
    backward = np.concatenate([np.cos(angle).T, -np.sin(angle).T], axis=1) / block

    def halves(table):
        high = table.astype(BF16)
        low = (table - high.astype(np.float64)).astype(BF16)
        return high, low

    f_high, f_low = halves(forward)
    b_high, b_low = halves(backward)
    return np.stack([f_high, f_low]), np.stack([b_high, b_low])


def dot(left, right):
    return jnp.dot(left, right, preferred_element_type=F32)


def conv_kernel(pair_ref, f_ref, b_ref, out_ref, spec, prod):
    nb, block, width2 = pair_ref.shape
    width = width2 // 2

    def ahead(p, carry):
        data = pair_ref[p]
        spec[p] = dot(f_ref[0], data) + dot(f_ref[1], data)
        return carry

    lax.fori_loop(0, nb, ahead, 0)

    rows = 8
    sign = 1.0 - 2.0 * (lax.broadcasted_iota(jnp.int32, (rows, width), 0) % 2).astype(F32)

    def products(chunk, carry):
        top = pl.multiple_of(chunk * rows, rows)
        re = pl.ds(top, rows)
        im = pl.ds(pl.multiple_of(block + top, rows), rows)
        x = [(spec[p, re, :width], spec[p, im, :width]) for p in range(nb)]
        h = [(spec[p, re, width:], spec[p, im, width:]) for p in range(nb)]
        last = None
        for j in range(nb):
            zr = zi = None
            for p in range(j + 1):
                xr, xi = x[p]
                hr, hi = h[j - p]
                tr = xr * hr - xi * hi
                ti = xr * hi + xi * hr
                zr = tr if zr is None else zr + tr
                zi = ti if zi is None else zi + ti
            if last is None:
                yr, yi = zr, zi
            else:
                yr = zr - sign * last[1]
                yi = zi + sign * last[0]
            last = (zr, zi)
            prod[j, re, :] = yr
            prod[j, im, :] = yi
        return carry

    lax.fori_loop(0, block // rows, products, 0)

    def back(j, carry):
        data = jnp.concatenate([prod[2 * j], prod[2 * j + 1]], axis=1)
        high = data.astype(BF16)
        low = (data - high.astype(F32)).astype(BF16)
        conv = (dot(b_ref[0], high) + (dot(b_ref[0], low) + dot(b_ref[1], high))).astype(BF16)
        out_ref[2 * j] = conv[:, :width]
        out_ref[2 * j + 1] = conv[:, width:]
        return carry

    lax.fori_loop(0, nb // 2, back, 0)


def causal_conv(pair):
    total, width2 = pair.shape
    width = width2 // 2
    nb = total // BLOCK
    forward, backward = transform_tables(BLOCK)
    out = pl.pallas_call(
        conv_kernel,
        out_shape=jax.ShapeDtypeStruct((nb, BLOCK, width), BF16),
        in_specs=[pl.BlockSpec(memory_space=pltpu.VMEM)] * 3,
        out_specs=pl.BlockSpec(memory_space=pltpu.VMEM),
        scratch_shapes=[
            pltpu.VMEM((nb, 2 * BLOCK, width2), F32),
            pltpu.VMEM((nb, 2 * BLOCK, width), F32),
        ],
        compiler_params=pltpu.CompilerParams(vmem_limit_bytes=48 * 1024 * 1024),
        cost_estimate=pl.CostEstimate(
            flops=14 * total * BLOCK * width2, bytes_accessed=6 * total * width, transcendentals=0
        ),
    )(pair.reshape(nb, BLOCK, width2), jnp.asarray(forward), jnp.asarray(backward))
    return out.reshape(total, width)


MESH = pl.DeviceIdType.MESH
CHUNKS = 8


def project_kernel(n_ch, g_ref, w_ref, out_ref, wx, gx, send, from_left, from_right, own,
                   w_send, w_recv, g_send, g_recv, send_sem, left_sem, right_sem):
    me = lax.axis_index("ch")
    chip = lax.div(me, 2)
    core = lax.rem(me, 2)
    mate = chip * 2 + 1 - core
    n_chip = n_ch // 2
    tokens, block = out_ref.shape
    rows = tokens // CHUNKS
    has_left = chip > 0
    has_right = chip < n_chip - 1
    left = jnp.maximum(me - 2, core)
    right = jnp.minimum(me + 2, n_ch - 2 + core)

    barrier = pltpu.get_barrier_semaphore()
    pl.semaphore_signal(barrier, inc=1, device_id={"ch": mate}, device_id_type=MESH)

    @pl.when(has_left)
    def _():
        pl.semaphore_signal(barrier, inc=1, device_id={"ch": left}, device_id_type=MESH)

    @pl.when(has_right)
    def _():
        pl.semaphore_signal(barrier, inc=1, device_id={"ch": right}, device_id_type=MESH)

    pl.semaphore_wait(barrier, 1 + has_left.astype(jnp.int32) + has_right.astype(jnp.int32))

    def columns(chip_at, core_at):
        return pl.ds(pl.multiple_of((chip_at * 2 + core_at) * block, block), block)

    def tokens_of(m):
        return pl.ds(pl.multiple_of(m * rows, rows), rows)

    def remote(src, dst, sent, arrived, target):
        return pltpu.make_async_remote_copy(
            src_ref=src, dst_ref=dst, send_sem=sent, recv_sem=arrived,
            device_id={"ch": target}, device_id_type=MESH,
        )

    def g_copy(m):
        at = tokens_of(m)
        return remote(g_ref.at[at], gx.at[at], g_send.at[m], g_recv.at[m], mate)

    def w_copy(t):
        return remote(w_ref.at[:, columns(t, 1 - core)], wx.at[t], w_send.at[t], w_recv.at[t], mate)

    def to_right(t, m):
        at = tokens_of(m)
        return remote(send.at[t, at], from_left.at[t, at], send_sem.at[t, m], left_sem.at[t, m], right)

    def to_left(t, m):
        at = tokens_of(m)
        return remote(send.at[t, at], from_right.at[t, at], send_sem.at[t, m], right_sem.at[t, m], left)

    def arrive_left(t, m):
        at = tokens_of(m)
        return remote(send.at[t, at], from_left.at[t, at], send_sem.at[t, m], left_sem.at[t, m], left)

    def arrive_right(t, m):
        at = tokens_of(m)
        return remote(send.at[t, at], from_right.at[t, at], send_sem.at[t, m], right_sem.at[t, m], right)

    for t in range(n_chip):
        w_copy(t).start()
    for m in range(CHUNKS):
        g_copy(m).start()
    for t in range(n_chip):
        w_copy(t).wait()

    def share(t, m):
        at = tokens_of(m)
        return dot(g_ref[at, :], w_ref[:, columns(t, core)]) + dot(gx[at, :], wx[t])

    def pass_on(t, m, first, arrived, copy):
        at = tokens_of(m)
        part = share(t, m)

        @pl.when(first)
        def _():
            send[t, at, :] = part.astype(BF16)

        @pl.when(jnp.logical_not(first))
        def _():
            arrived(t, m)

        @pl.when(jnp.logical_not(first))
        def _():
            buffer = from_left if copy is to_right else from_right
            send[t, at, :] = (part + buffer[t, at, :].astype(F32)).astype(BF16)

        copy(t, m).start()

    def drain(m):
        for d in range(n_chip - 1, 0, -1):
            @pl.when(chip + d < n_chip)
            def _():
                to_right(chip + d, m).wait_send()

            @pl.when(chip - d >= 0)
            def _():
                to_left(chip - d, m).wait_send()

    def step(m, carry):
        g_copy(m).wait()

        @pl.when(m >= 2)
        def _():
            drain(m - 2)

        for d in range(n_chip - 1, 0, -1):
            @pl.when(chip + d < n_chip)
            def _():
                pass_on(chip + d, m, jnp.logical_not(has_left),
                        lambda t, m: arrive_left(t, m).wait_recv(), to_right)

            @pl.when(chip - d >= 0)
            def _():
                pass_on(chip - d, m, jnp.logical_not(has_right),
                        lambda t, m: arrive_right(t, m).wait_recv(), to_left)

        own[tokens_of(m), :] = share(chip, m)
        return carry

    lax.fori_loop(0, CHUNKS, step, 0)

    def finish(m, carry):
        at = tokens_of(m)

        @pl.when(has_left)
        def _():
            arrive_left(chip, m).wait_recv()
            own[at, :] += from_left[chip, at, :].astype(F32)

        @pl.when(has_right)
        def _():
            arrive_right(chip, m).wait_recv()
            own[at, :] += from_right[chip, at, :].astype(F32)

        out_ref[at, :] = own[at, :].astype(BF16)
        return carry

    lax.fori_loop(0, CHUNKS, finish, 0)
    drain(CHUNKS - 2)
    drain(CHUNKS - 1)


def project(gated, out_weight):
    tokens, channels = gated.shape
    n_ch = lax.axis_size("ch")
    n_chip = n_ch // 2
    block = out_weight.shape[1] // n_ch
    return pl.pallas_call(
        functools.partial(project_kernel, n_ch),
        out_shape=jax.ShapeDtypeStruct((tokens, block), BF16),
        in_specs=[pl.BlockSpec(memory_space=pltpu.VMEM)] * 2,
        out_specs=pl.BlockSpec(memory_space=pltpu.VMEM),
        scratch_shapes=[
            pltpu.VMEM((n_chip, channels, block), BF16),
            pltpu.VMEM((tokens, channels), BF16),
            pltpu.VMEM((n_chip, tokens, block), BF16),
            pltpu.VMEM((n_chip, tokens, block), BF16),
            pltpu.VMEM((n_chip, tokens, block), BF16),
            pltpu.VMEM((tokens, block), F32),
            pltpu.SemaphoreType.DMA((n_chip,)),
            pltpu.SemaphoreType.DMA((n_chip,)),
            pltpu.SemaphoreType.DMA((CHUNKS,)),
            pltpu.SemaphoreType.DMA((CHUNKS,)),
            pltpu.SemaphoreType.DMA((n_chip, CHUNKS)),
            pltpu.SemaphoreType.DMA((n_chip, CHUNKS)),
            pltpu.SemaphoreType.DMA((n_chip, CHUNKS)),
        ],
        compiler_params=pltpu.CompilerParams(
            collective_id=0, has_side_effects=True, vmem_limit_bytes=48 * 1024 * 1024
        ),
        cost_estimate=pl.CostEstimate(
            flops=2 * tokens * channels * n_ch * block,
            bytes_accessed=2 * channels * n_ch * block, transcendentals=0,
        ),
    )(gated, out_weight)


def per_device(queries, key_input, value_input, filters, skip_gain, out_weight):
    tok_rows, channels = queries.shape
    n_ctx = lax.axis_size("ctx")
    width = channels // n_ctx
    mixed_in = (key_input.astype(F32) * value_input.astype(F32)).astype(BF16)
    split = lambda a: a.reshape(tok_rows, n_ctx, width)
    pair = jnp.concatenate([split(mixed_in), split(filters)], axis=2).transpose(1, 0, 2)
    pair = lax.all_to_all(pair, "ctx", 0, 0, tiled=True)
    conv = causal_conv(pair.reshape(n_ctx * tok_rows, 2 * width))
    conv = lax.all_to_all(conv.reshape(n_ctx, tok_rows, width), "ctx", 0, 0, tiled=True)
    conv = conv.transpose(1, 0, 2).reshape(tok_rows, channels).astype(F32)
    gated = (
        queries.astype(F32) * (conv + skip_gain[None, :] * mixed_in.astype(F32))
    ).astype(BF16)
    return project(gated, out_weight)


def solution(mesh):
    in_specs = (
        P("ctx", "ch"),
        P("ctx", "ch"),
        P("ctx", "ch"),
        P("ctx", "ch"),
        P("ch"),
        P("ch", None),
    )
    return jax.shard_map(
        per_device, mesh=mesh, in_specs=in_specs, out_specs=P("ctx", "ch"), check_vma=False
    )
```

```python
import functools

import jax
import jax.numpy as jnp
import numpy as np
from jax import lax
from jax.experimental import pallas as pl
from jax.experimental.pallas import tpu as pltpu
from jax.sharding import PartitionSpec as P

BLOCK = 256
F32 = jnp.float32
BF16 = jnp.bfloat16


def transform_tables(block):
    k = np.arange(block)[:, None]
    n = np.arange(block)[None, :]
    angle = np.pi * (((2 * k + 1) * n) % (4 * block)) / (2 * block)
    forward = np.concatenate([np.cos(angle), -np.sin(angle)], axis=0)
    backward = np.concatenate([np.cos(angle).T, -np.sin(angle).T], axis=1) / block

    def halves(table):
        high = table.astype(BF16)
        low = (table - high.astype(np.float64)).astype(BF16)
        return high, low

    f_high, f_low = halves(forward)
    b_high, b_low = halves(backward)
    return np.stack([f_high, f_low]), np.stack([b_high, b_low])


def dot(left, right):
    return jnp.dot(left, right, preferred_element_type=F32)


MESH = pl.DeviceIdType.MESH


def gate_kernel(n_ctx, q_ref, k_ref, v_ref, h_ref, skip_ref, f_ref, b_ref, w_ref, out_ref, wx,
                outbox, inbox, spec, prod, conv_out, conv_in,
                w_send, w_recv, in_send, in_recv, back_send, back_recv):
    me = lax.axis_index("ctx")
    ch = lax.axis_index("ch")
    core = lax.rem(ch, 2)
    mate = ch + 1 - 2 * core
    n_chip, _, wide = wx.shape
    tokens = q_ref.shape[0]
    width = conv_in.shape[2]
    block = BLOCK
    per = tokens // block
    nb = n_ctx * per

    barrier = pltpu.get_barrier_semaphore()
    pl.semaphore_signal(barrier, inc=1, device_id={"ch": mate}, device_id_type=MESH)
    for d in range(1, n_ctx):
        pl.semaphore_signal(
            barrier, inc=1, device_id={"ctx": lax.rem(me + d, n_ctx)}, device_id_type=MESH
        )

    def rows_of(r):
        return pl.ds(pl.multiple_of(r * block, block), block)

    def fill(r, carry):
        at = rows_of(r)
        for i in range(n_ctx):
            lanes = slice(i * width, (i + 1) * width)
            mixed = k_ref[at, lanes].astype(F32) * v_ref[at, lanes].astype(F32)
            outbox[i, at, :width] = mixed.astype(BF16)
            outbox[i, at, width:] = h_ref[at, lanes]
        return carry

    lax.fori_loop(0, per, fill, 0)
    pl.semaphore_wait(barrier, n_ctx)

    def in_copy(d):
        to = lax.rem(me + d, n_ctx)
        return pltpu.make_async_remote_copy(
            src_ref=outbox.at[to], dst_ref=inbox.at[me],
            send_sem=in_send.at[d], recv_sem=in_recv.at[d],
            device_id={"ctx": to}, device_id_type=MESH,
        )

    def in_wait(d):
        source = lax.rem(me + n_ctx - d, n_ctx)
        pltpu.make_async_remote_copy(
            src_ref=outbox.at[source], dst_ref=inbox.at[source],
            send_sem=in_send.at[d], recv_sem=in_recv.at[d],
            device_id={"ctx": source}, device_id_type=MESH,
        ).wait_recv()

    def back_copy(d):
        to = lax.rem(me + d, n_ctx)
        return pltpu.make_async_remote_copy(
            src_ref=conv_out.at[to], dst_ref=conv_in.at[me],
            send_sem=back_send.at[d], recv_sem=back_recv.at[d],
            device_id={"ctx": to}, device_id_type=MESH,
        )

    def back_wait(d):
        source = lax.rem(me + n_ctx - d, n_ctx)
        pltpu.make_async_remote_copy(
            src_ref=conv_out.at[source], dst_ref=conv_in.at[source],
            send_sem=back_send.at[d], recv_sem=back_recv.at[d],
            device_id={"ctx": source}, device_id_type=MESH,
        ).wait_recv()

    def w_copy(t):
        lanes = pl.ds(pl.multiple_of((t * 2 + 1 - core) * wide, wide), wide)
        return pltpu.make_async_remote_copy(
            src_ref=w_ref.at[:, lanes], dst_ref=wx.at[t],
            send_sem=w_send.at[t], recv_sem=w_recv.at[t],
            device_id={"ch": mate}, device_id_type=MESH,
        )

    for d in range(1, n_ctx):
        in_copy(d).start()
    for t in range(n_chip):
        w_copy(t).start()

    def ahead(box, source):
        def one(r, carry):
            data = box[source, rows_of(r), :]
            spec[source * per + r] = dot(f_ref[0], data) + dot(f_ref[1], data)
            return carry

        lax.fori_loop(0, per, one, 0)

    ahead(outbox, me)
    for d in range(1, n_ctx):
        in_wait(d)
        ahead(inbox, lax.rem(me + n_ctx - d, n_ctx))

    rows = 8
    sign = 1.0 - 2.0 * (lax.broadcasted_iota(jnp.int32, (rows, width), 0) % 2).astype(F32)

    def products(chunk, carry):
        top = pl.multiple_of(chunk * rows, rows)
        re = pl.ds(top, rows)
        im = pl.ds(pl.multiple_of(block + top, rows), rows)
        x = [(spec[p, re, :width], spec[p, im, :width]) for p in range(nb)]
        h = [(spec[p, re, width:], spec[p, im, width:]) for p in range(nb)]
        last = None
        for j in range(nb):
            zr = zi = None
            for p in range(j + 1):
                xr, xi = x[p]
                hr, hi = h[j - p]
                tr = xr * hr - xi * hi
                ti = xr * hi + xi * hr
                zr = tr if zr is None else zr + tr
                zi = ti if zi is None else zi + ti
            if last is None:
                yr, yi = zr, zi
            else:
                yr = zr - sign * last[1]
                yi = zi + sign * last[0]
            last = (zr, zi)
            prod[j, re, :] = yr
            prod[j, im, :] = yi
        return carry

    lax.fori_loop(0, block // rows, products, 0)

    def back(box, to):
        def one(r, carry):
            j = to * per + 2 * r
            data = jnp.concatenate([prod[j], prod[j + 1]], axis=1)
            high = data.astype(BF16)
            low = (data - high.astype(F32)).astype(BF16)
            conv = (dot(b_ref[0], high) + (dot(b_ref[0], low) + dot(b_ref[1], high))).astype(BF16)
            box[to, rows_of(2 * r), :] = conv[:, :width]
            box[to, rows_of(2 * r + 1), :] = conv[:, width:]
            return carry

        lax.fori_loop(0, per // 2, one, 0)

    for d in range(1, n_ctx):
        back(conv_out, lax.rem(me + d, n_ctx))
        back_copy(d).start()
    back(conv_in, me)
    for d in range(1, n_ctx):
        back_wait(d)

    def gate(r, carry):
        at = rows_of(r)
        for i in range(n_ctx):
            lanes = slice(i * width, (i + 1) * width)
            mixed = outbox[i, at, :width].astype(F32)
            total = conv_in[i, at, :].astype(F32) + skip_ref[:, lanes] * mixed
            out_ref[at, lanes] = (q_ref[at, lanes].astype(F32) * total).astype(BF16)
        return carry

    lax.fori_loop(0, per, gate, 0)
    for d in range(1, n_ctx):
        in_copy(d).wait_send()
        back_copy(d).wait_send()
    for t in range(n_chip):
        w_copy(t).wait()


def gated_conv(queries, key_input, value_input, filters, skip_gain, out_weight):
    tokens, channels = queries.shape
    n_ctx = lax.axis_size("ctx")
    n_ch = lax.axis_size("ch")
    n_chip = n_ch // 2
    width = channels // n_ctx
    nb = n_ctx * tokens // BLOCK
    forward, backward = transform_tables(BLOCK)
    vmem = pl.BlockSpec(memory_space=pltpu.VMEM)
    hbm = pl.BlockSpec(memory_space=pl.ANY)
    return pl.pallas_call(
        functools.partial(gate_kernel, n_ctx),
        out_shape=(
            jax.ShapeDtypeStruct((tokens, channels), BF16),
            jax.ShapeDtypeStruct((n_chip, channels, out_weight.shape[1] // n_ch), BF16),
        ),
        in_specs=[vmem] * 7 + [hbm],
        out_specs=(vmem, hbm),
        scratch_shapes=[
            pltpu.VMEM((n_ctx, tokens, 2 * width), BF16),
            pltpu.VMEM((n_ctx, tokens, 2 * width), BF16),
            pltpu.VMEM((nb, 2 * BLOCK, 2 * width), F32),
            pltpu.VMEM((nb, 2 * BLOCK, width), F32),
            pltpu.VMEM((n_ctx, tokens, width), BF16),
            pltpu.VMEM((n_ctx, tokens, width), BF16),
            pltpu.SemaphoreType.DMA((n_chip,)),
            pltpu.SemaphoreType.DMA((n_chip,)),
            pltpu.SemaphoreType.DMA((n_ctx,)),
            pltpu.SemaphoreType.DMA((n_ctx,)),
            pltpu.SemaphoreType.DMA((n_ctx,)),
            pltpu.SemaphoreType.DMA((n_ctx,)),
        ],
        compiler_params=pltpu.CompilerParams(
            collective_id=1, has_side_effects=True, vmem_limit_bytes=56 * 1024 * 1024
        ),
        cost_estimate=pl.CostEstimate(
            flops=28 * n_ctx * tokens * BLOCK * width, bytes_accessed=10 * tokens * channels,
            transcendentals=0,
        ),
    )(queries, key_input, value_input, filters, skip_gain[None, :],
      jnp.asarray(forward), jnp.asarray(backward), out_weight)


CHUNKS = 8


def project_kernel(n_ch, g_ref, w_ref, wx, out_ref, gx, send, from_left, from_right, own,
                   g_send, g_recv, send_sem, left_sem, right_sem):
    me = lax.axis_index("ch")
    chip = lax.div(me, 2)
    core = lax.rem(me, 2)
    mate = chip * 2 + 1 - core
    n_chip = n_ch // 2
    tokens, block = out_ref.shape
    rows = tokens // CHUNKS
    has_left = chip > 0
    has_right = chip < n_chip - 1
    left = jnp.maximum(me - 2, core)
    right = jnp.minimum(me + 2, n_ch - 2 + core)

    barrier = pltpu.get_barrier_semaphore()
    pl.semaphore_signal(barrier, inc=1, device_id={"ch": mate}, device_id_type=MESH)

    @pl.when(has_left)
    def _():
        pl.semaphore_signal(barrier, inc=1, device_id={"ch": left}, device_id_type=MESH)

    @pl.when(has_right)
    def _():
        pl.semaphore_signal(barrier, inc=1, device_id={"ch": right}, device_id_type=MESH)

    pl.semaphore_wait(barrier, 1 + has_left.astype(jnp.int32) + has_right.astype(jnp.int32))

    def columns(chip_at, core_at):
        return pl.ds(pl.multiple_of((chip_at * 2 + core_at) * block, block), block)

    def tokens_of(m):
        return pl.ds(pl.multiple_of(m * rows, rows), rows)

    def remote(src, dst, sent, arrived, target):
        return pltpu.make_async_remote_copy(
            src_ref=src, dst_ref=dst, send_sem=sent, recv_sem=arrived,
            device_id={"ch": target}, device_id_type=MESH,
        )

    def g_copy(m):
        at = tokens_of(m)
        return remote(g_ref.at[at], gx.at[at], g_send.at[m], g_recv.at[m], mate)

    def to_right(t, m):
        at = tokens_of(m)
        return remote(send.at[t, at], from_left.at[t, at], send_sem.at[t, m], left_sem.at[t, m], right)

    def to_left(t, m):
        at = tokens_of(m)
        return remote(send.at[t, at], from_right.at[t, at], send_sem.at[t, m], right_sem.at[t, m], left)

    def arrive_left(t, m):
        at = tokens_of(m)
        return remote(send.at[t, at], from_left.at[t, at], send_sem.at[t, m], left_sem.at[t, m], left)

    def arrive_right(t, m):
        at = tokens_of(m)
        return remote(send.at[t, at], from_right.at[t, at], send_sem.at[t, m], right_sem.at[t, m], right)

    for m in range(CHUNKS):
        g_copy(m).start()

    def share(t, m):
        at = tokens_of(m)
        return dot(g_ref[at, :], w_ref[:, columns(t, core)]) + dot(gx[at, :], wx[t])

    def pass_on(t, m, first, arrived, copy):
        at = tokens_of(m)
        part = share(t, m)

        @pl.when(first)
        def _():
            send[t, at, :] = part.astype(BF16)

        @pl.when(jnp.logical_not(first))
        def _():
            arrived(t, m)

        @pl.when(jnp.logical_not(first))
        def _():
            buffer = from_left if copy is to_right else from_right
            send[t, at, :] = (part + buffer[t, at, :].astype(F32)).astype(BF16)

        copy(t, m).start()

    def drain(m):
        for d in range(n_chip - 1, 0, -1):
            @pl.when(chip + d < n_chip)
            def _():
                to_right(chip + d, m).wait_send()

            @pl.when(chip - d >= 0)
            def _():
                to_left(chip - d, m).wait_send()

    def step(m, carry):
        g_copy(m).wait()

        @pl.when(m >= 2)
        def _():
            drain(m - 2)

        for d in range(n_chip - 1, 0, -1):
            @pl.when(chip + d < n_chip)
            def _():
                pass_on(chip + d, m, jnp.logical_not(has_left),
                        lambda t, m: arrive_left(t, m).wait_recv(), to_right)

            @pl.when(chip - d >= 0)
            def _():
                pass_on(chip - d, m, jnp.logical_not(has_right),
                        lambda t, m: arrive_right(t, m).wait_recv(), to_left)

        own[tokens_of(m), :] = share(chip, m)
        return carry

    lax.fori_loop(0, CHUNKS, step, 0)

    def finish(m, carry):
        at = tokens_of(m)

        @pl.when(has_left)
        def _():
            arrive_left(chip, m).wait_recv()
            own[at, :] += from_left[chip, at, :].astype(F32)

        @pl.when(has_right)
        def _():
            arrive_right(chip, m).wait_recv()
            own[at, :] += from_right[chip, at, :].astype(F32)

        out_ref[at, :] = own[at, :].astype(BF16)
        return carry

    lax.fori_loop(0, CHUNKS, finish, 0)
    drain(CHUNKS - 2)
    drain(CHUNKS - 1)


def project(gated, out_weight, mate_weight):
    tokens, channels = gated.shape
    n_ch = lax.axis_size("ch")
    n_chip = n_ch // 2
    block = out_weight.shape[1] // n_ch
    return pl.pallas_call(
        functools.partial(project_kernel, n_ch),
        out_shape=jax.ShapeDtypeStruct((tokens, block), BF16),
        in_specs=[pl.BlockSpec(memory_space=pltpu.VMEM)] * 3,
        out_specs=pl.BlockSpec(memory_space=pltpu.VMEM),
        scratch_shapes=[
            pltpu.VMEM((tokens, channels), BF16),
            pltpu.VMEM((n_chip, tokens, block), BF16),
            pltpu.VMEM((n_chip, tokens, block), BF16),
            pltpu.VMEM((n_chip, tokens, block), BF16),
            pltpu.VMEM((tokens, block), F32),
            pltpu.SemaphoreType.DMA((CHUNKS,)),
            pltpu.SemaphoreType.DMA((CHUNKS,)),
            pltpu.SemaphoreType.DMA((n_chip, CHUNKS)),
            pltpu.SemaphoreType.DMA((n_chip, CHUNKS)),
            pltpu.SemaphoreType.DMA((n_chip, CHUNKS)),
        ],
        compiler_params=pltpu.CompilerParams(
            collective_id=0, has_side_effects=True, vmem_limit_bytes=48 * 1024 * 1024
        ),
        cost_estimate=pl.CostEstimate(
            flops=2 * tokens * channels * n_ch * block,
            bytes_accessed=2 * channels * n_ch * block, transcendentals=0,
        ),
    )(gated, out_weight, mate_weight)


def per_device(queries, key_input, value_input, filters, skip_gain, out_weight):
    gated, mate_weight = gated_conv(
        queries, key_input, value_input, filters, skip_gain, out_weight
    )
    return project(gated, out_weight, mate_weight)


def solution(mesh):
    in_specs = (
        P("ctx", "ch"),
        P("ctx", "ch"),
        P("ctx", "ch"),
        P("ctx", "ch"),
        P("ch"),
        P("ch", None),
    )
    return jax.shard_map(
        per_device, mesh=mesh, in_specs=in_specs, out_specs=P("ctx", "ch"), check_vma=False
    )
```

```python
import functools

import jax
import jax.numpy as jnp
import numpy as np
from jax import lax
from jax.experimental import pallas as pl
from jax.experimental.pallas import tpu as pltpu
from jax.sharding import PartitionSpec as P

BLOCK = 256
F32 = jnp.float32
BF16 = jnp.bfloat16


def transform_tables(block):
    k = np.arange(block)[:, None]
    n = np.arange(block)[None, :]
    angle = np.pi * (((2 * k + 1) * n) % (4 * block)) / (2 * block)
    forward = np.concatenate([np.cos(angle), -np.sin(angle)], axis=0)
    backward = np.concatenate([np.cos(angle).T, -np.sin(angle).T], axis=1) / block

    def halves(table):
        high = table.astype(BF16)
        low = (table - high.astype(np.float64)).astype(BF16)
        return high, low

    f_high, f_low = halves(forward)
    b_high, b_low = halves(backward)
    return np.stack([f_high, f_low]), np.stack([b_high, b_low])


def dot(left, right):
    return jnp.dot(left, right, preferred_element_type=F32)


MESH = pl.DeviceIdType.MESH


def gate_kernel(n_ctx, q_ref, k_ref, v_ref, h_ref, skip_ref, f_ref, b_ref, w_ref, out_ref, wx,
                outbox, inbox, spec, prod, conv_out, conv_in,
                w_send, w_recv, in_send, in_recv, back_send, back_recv):
    me = lax.axis_index("ctx")
    ch = lax.axis_index("ch")
    core = lax.rem(ch, 2)
    mate = ch + 1 - 2 * core
    n_chip, _, wide = wx.shape
    tokens = q_ref.shape[0]
    width = conv_in.shape[2]
    block = BLOCK
    per = tokens // block
    nb = n_ctx * per

    barrier = pltpu.get_barrier_semaphore()
    pl.semaphore_signal(barrier, inc=1, device_id={"ch": mate}, device_id_type=MESH)
    for d in range(1, n_ctx):
        pl.semaphore_signal(
            barrier, inc=1, device_id={"ctx": lax.rem(me + d, n_ctx)}, device_id_type=MESH
        )

    def rows_of(r):
        return pl.ds(pl.multiple_of(r * block, block), block)

    def fill(r, carry):
        at = rows_of(r)
        for i in range(n_ctx):
            lanes = slice(i * width, (i + 1) * width)
            mixed = k_ref[at, lanes].astype(F32) * v_ref[at, lanes].astype(F32)
            outbox[i, at, :width] = mixed.astype(BF16)
            outbox[i, at, width:] = h_ref[at, lanes]
        return carry

    lax.fori_loop(0, per, fill, 0)
    pl.semaphore_wait(barrier, n_ctx)

    def in_copy(d):
        to = lax.rem(me + d, n_ctx)
        return pltpu.make_async_remote_copy(
            src_ref=outbox.at[to], dst_ref=inbox.at[me],
            send_sem=in_send.at[d], recv_sem=in_recv.at[d],
            device_id={"ctx": to}, device_id_type=MESH,
        )

    def in_wait(d):
        source = lax.rem(me + n_ctx - d, n_ctx)
        pltpu.make_async_remote_copy(
            src_ref=outbox.at[source], dst_ref=inbox.at[source],
            send_sem=in_send.at[d], recv_sem=in_recv.at[d],
            device_id={"ctx": source}, device_id_type=MESH,
        ).wait_recv()

    def back_copy(d):
        to = lax.rem(me + d, n_ctx)
        return pltpu.make_async_remote_copy(
            src_ref=conv_out.at[to], dst_ref=conv_in.at[me],
            send_sem=back_send.at[d], recv_sem=back_recv.at[d],
            device_id={"ctx": to}, device_id_type=MESH,
        )

    def back_wait(d):
        source = lax.rem(me + n_ctx - d, n_ctx)
        pltpu.make_async_remote_copy(
            src_ref=conv_out.at[source], dst_ref=conv_in.at[source],
            send_sem=back_send.at[d], recv_sem=back_recv.at[d],
            device_id={"ctx": source}, device_id_type=MESH,
        ).wait_recv()

    def w_copy(t):
        lanes = pl.ds(pl.multiple_of((t * 2 + 1 - core) * wide, wide), wide)
        return pltpu.make_async_remote_copy(
            src_ref=w_ref.at[:, lanes], dst_ref=wx.at[t],
            send_sem=w_send.at[t], recv_sem=w_recv.at[t],
            device_id={"ch": mate}, device_id_type=MESH,
        )

    for d in range(1, n_ctx):
        in_copy(d).start()
    for t in range(n_chip):
        w_copy(t).start()

    def ahead(box, source):
        def one(r, carry):
            data = box[source, rows_of(r), :]
            spec[source * per + r] = dot(f_ref[0], data) + dot(f_ref[1], data)
            return carry

        lax.fori_loop(0, per, one, 0)

    ahead(outbox, me)
    for d in range(1, n_ctx):
        in_wait(d)
        ahead(inbox, lax.rem(me + n_ctx - d, n_ctx))

    rows = 8
    sign = 1.0 - 2.0 * (lax.broadcasted_iota(jnp.int32, (rows, width), 0) % 2).astype(F32)

    def products(chunk, carry):
        top = pl.multiple_of(chunk * rows, rows)
        re = pl.ds(top, rows)
        im = pl.ds(pl.multiple_of(block + top, rows), rows)
        x = [(spec[p, re, :width], spec[p, im, :width]) for p in range(nb)]
        h = [(spec[p, re, width:], spec[p, im, width:]) for p in range(nb)]
        last = None
        for j in range(nb):
            zr = zi = None
            for p in range(j + 1):
                xr, xi = x[p]
                hr, hi = h[j - p]
                tr = xr * hr - xi * hi
                ti = xr * hi + xi * hr
                zr = tr if zr is None else zr + tr
                zi = ti if zi is None else zi + ti
            if last is None:
                yr, yi = zr, zi
            else:
                yr = zr - sign * last[1]
                yi = zi + sign * last[0]
            last = (zr, zi)
            prod[j, re, :] = yr
            prod[j, im, :] = yi
        return carry

    lax.fori_loop(0, block // rows, products, 0)

    def back(box, to):
        def one(r, carry):
            j = to * per + 2 * r
            data = jnp.concatenate([prod[j], prod[j + 1]], axis=1)
            high = data.astype(BF16)
            low = (data - high.astype(F32)).astype(BF16)
            conv = (dot(b_ref[0], high) + (dot(b_ref[0], low) + dot(b_ref[1], high))).astype(BF16)
            box[to, rows_of(2 * r), :] = conv[:, :width]
            box[to, rows_of(2 * r + 1), :] = conv[:, width:]
            return carry

        lax.fori_loop(0, per // 2, one, 0)

    for d in range(1, n_ctx):
        back(conv_out, lax.rem(me + d, n_ctx))
        back_copy(d).start()
    back(conv_in, me)
    for d in range(1, n_ctx):
        back_wait(d)

    def gate(r, carry):
        at = rows_of(r)
        for i in range(n_ctx):
            lanes = slice(i * width, (i + 1) * width)
            mixed = outbox[i, at, :width].astype(F32)
            total = conv_in[i, at, :].astype(F32) + skip_ref[:, lanes] * mixed
            out_ref[at, lanes] = (q_ref[at, lanes].astype(F32) * total).astype(BF16)
        return carry

    lax.fori_loop(0, per, gate, 0)
    for d in range(1, n_ctx):
        in_copy(d).wait_send()
        back_copy(d).wait_send()
    for t in range(n_chip):
        w_copy(t).wait()


def gated_conv(queries, key_input, value_input, filters, skip_gain, out_weight):
    tokens, channels = queries.shape
    n_ctx = lax.axis_size("ctx")
    n_ch = lax.axis_size("ch")
    n_chip = n_ch // 2
    width = channels // n_ctx
    nb = n_ctx * tokens // BLOCK
    forward, backward = transform_tables(BLOCK)
    vmem = pl.BlockSpec(memory_space=pltpu.VMEM)
    hbm = pl.BlockSpec(memory_space=pl.ANY)
    return pl.pallas_call(
        functools.partial(gate_kernel, n_ctx),
        out_shape=(
            jax.ShapeDtypeStruct((tokens, channels), BF16),
            jax.ShapeDtypeStruct((n_chip, channels, out_weight.shape[1] // n_ch), BF16),
        ),
        in_specs=[vmem] * 7 + [hbm],
        out_specs=(vmem, hbm),
        scratch_shapes=[
            pltpu.VMEM((n_ctx, tokens, 2 * width), BF16),
            pltpu.VMEM((n_ctx, tokens, 2 * width), BF16),
            pltpu.VMEM((nb, 2 * BLOCK, 2 * width), F32),
            pltpu.VMEM((nb, 2 * BLOCK, width), F32),
            pltpu.VMEM((n_ctx, tokens, width), BF16),
            pltpu.VMEM((n_ctx, tokens, width), BF16),
            pltpu.SemaphoreType.DMA((n_chip,)),
            pltpu.SemaphoreType.DMA((n_chip,)),
            pltpu.SemaphoreType.DMA((n_ctx,)),
            pltpu.SemaphoreType.DMA((n_ctx,)),
            pltpu.SemaphoreType.DMA((n_ctx,)),
            pltpu.SemaphoreType.DMA((n_ctx,)),
        ],
        compiler_params=pltpu.CompilerParams(
            collective_id=1, has_side_effects=True, vmem_limit_bytes=56 * 1024 * 1024
        ),
        cost_estimate=pl.CostEstimate(
            flops=28 * n_ctx * tokens * BLOCK * width, bytes_accessed=10 * tokens * channels,
            transcendentals=0,
        ),
    )(queries, key_input, value_input, filters, skip_gain[None, :],
      jnp.asarray(forward), jnp.asarray(backward), out_weight)


CHUNKS = 4


def project_kernel(n_ch, g_ref, w_ref, wx, out_ref, gx, send, from_left, from_right, own,
                   g_send, g_recv, send_sem, left_sem, right_sem):
    me = lax.axis_index("ch")
    chip = lax.div(me, 2)
    core = lax.rem(me, 2)
    mate = chip * 2 + 1 - core
    n_chip = n_ch // 2
    tokens, block = out_ref.shape
    rows = tokens // CHUNKS
    has_left = chip > 0
    has_right = chip < n_chip - 1
    left = jnp.maximum(me - 2, core)
    right = jnp.minimum(me + 2, n_ch - 2 + core)

    barrier = pltpu.get_barrier_semaphore()
    pl.semaphore_signal(barrier, inc=1, device_id={"ch": mate}, device_id_type=MESH)

    @pl.when(has_left)
    def _():
        pl.semaphore_signal(barrier, inc=1, device_id={"ch": left}, device_id_type=MESH)

    @pl.when(has_right)
    def _():
        pl.semaphore_signal(barrier, inc=1, device_id={"ch": right}, device_id_type=MESH)

    pl.semaphore_wait(barrier, 1 + has_left.astype(jnp.int32) + has_right.astype(jnp.int32))

    def columns(chip_at, core_at):
        return pl.ds(pl.multiple_of((chip_at * 2 + core_at) * block, block), block)

    def tokens_of(m):
        return pl.ds(pl.multiple_of(m * rows, rows), rows)

    def remote(src, dst, sent, arrived, target):
        return pltpu.make_async_remote_copy(
            src_ref=src, dst_ref=dst, send_sem=sent, recv_sem=arrived,
            device_id={"ch": target}, device_id_type=MESH,
        )

    def g_copy(m):
        at = tokens_of(m)
        return remote(g_ref.at[at], gx.at[at], g_send.at[m], g_recv.at[m], mate)

    def to_right(t, m):
        at = tokens_of(m)
        return remote(send.at[t, at], from_left.at[t, at], send_sem.at[t, m], left_sem.at[t, m], right)

    def to_left(t, m):
        at = tokens_of(m)
        return remote(send.at[t, at], from_right.at[t, at], send_sem.at[t, m], right_sem.at[t, m], left)

    def arrive_left(t, m):
        at = tokens_of(m)
        return remote(send.at[t, at], from_left.at[t, at], send_sem.at[t, m], left_sem.at[t, m], left)

    def arrive_right(t, m):
        at = tokens_of(m)
        return remote(send.at[t, at], from_right.at[t, at], send_sem.at[t, m], right_sem.at[t, m], right)

    for m in range(CHUNKS):
        g_copy(m).start()

    def share(t, m):
        at = tokens_of(m)
        return dot(g_ref[at, :], w_ref[:, columns(t, core)]) + dot(gx[at, :], wx[t])

    def pass_on(t, m, first, arrived, copy):
        at = tokens_of(m)
        part = share(t, m)

        @pl.when(first)
        def _():
            send[t, at, :] = part.astype(BF16)

        @pl.when(jnp.logical_not(first))
        def _():
            arrived(t, m)

        @pl.when(jnp.logical_not(first))
        def _():
            buffer = from_left if copy is to_right else from_right
            send[t, at, :] = (part + buffer[t, at, :].astype(F32)).astype(BF16)

        copy(t, m).start()

    def drain(m):
        for d in range(n_chip - 1, 0, -1):
            @pl.when(chip + d < n_chip)
            def _():
                to_right(chip + d, m).wait_send()

            @pl.when(chip - d >= 0)
            def _():
                to_left(chip - d, m).wait_send()

    def step(m, carry):
        g_copy(m).wait()

        @pl.when(m >= 2)
        def _():
            drain(m - 2)

        for d in range(n_chip - 1, 0, -1):
            @pl.when(chip + d < n_chip)
            def _():
                pass_on(chip + d, m, jnp.logical_not(has_left),
                        lambda t, m: arrive_left(t, m).wait_recv(), to_right)

            @pl.when(chip - d >= 0)
            def _():
                pass_on(chip - d, m, jnp.logical_not(has_right),
                        lambda t, m: arrive_right(t, m).wait_recv(), to_left)

        own[tokens_of(m), :] = share(chip, m)
        return carry

    lax.fori_loop(0, CHUNKS, step, 0)

    def finish(m, carry):
        at = tokens_of(m)

        @pl.when(has_left)
        def _():
            arrive_left(chip, m).wait_recv()
            own[at, :] += from_left[chip, at, :].astype(F32)

        @pl.when(has_right)
        def _():
            arrive_right(chip, m).wait_recv()
            own[at, :] += from_right[chip, at, :].astype(F32)

        out_ref[at, :] = own[at, :].astype(BF16)
        return carry

    lax.fori_loop(0, CHUNKS, finish, 0)
    drain(CHUNKS - 2)
    drain(CHUNKS - 1)


def project(gated, out_weight, mate_weight):
    tokens, channels = gated.shape
    n_ch = lax.axis_size("ch")
    n_chip = n_ch // 2
    block = out_weight.shape[1] // n_ch
    return pl.pallas_call(
        functools.partial(project_kernel, n_ch),
        out_shape=jax.ShapeDtypeStruct((tokens, block), BF16),
        in_specs=[pl.BlockSpec(memory_space=pltpu.VMEM)] * 3,
        out_specs=pl.BlockSpec(memory_space=pltpu.VMEM),
        scratch_shapes=[
            pltpu.VMEM((tokens, channels), BF16),
            pltpu.VMEM((n_chip, tokens, block), BF16),
            pltpu.VMEM((n_chip, tokens, block), BF16),
            pltpu.VMEM((n_chip, tokens, block), BF16),
            pltpu.VMEM((tokens, block), F32),
            pltpu.SemaphoreType.DMA((CHUNKS,)),
            pltpu.SemaphoreType.DMA((CHUNKS,)),
            pltpu.SemaphoreType.DMA((n_chip, CHUNKS)),
            pltpu.SemaphoreType.DMA((n_chip, CHUNKS)),
            pltpu.SemaphoreType.DMA((n_chip, CHUNKS)),
        ],
        compiler_params=pltpu.CompilerParams(
            collective_id=0, has_side_effects=True, vmem_limit_bytes=48 * 1024 * 1024
        ),
        cost_estimate=pl.CostEstimate(
            flops=2 * tokens * channels * n_ch * block,
            bytes_accessed=2 * channels * n_ch * block, transcendentals=0,
        ),
    )(gated, out_weight, mate_weight)


def per_device(queries, key_input, value_input, filters, skip_gain, out_weight):
    gated, mate_weight = gated_conv(
        queries, key_input, value_input, filters, skip_gain, out_weight
    )
    return project(gated, out_weight, mate_weight)


def solution(mesh):
    in_specs = (
        P("ctx", "ch"),
        P("ctx", "ch"),
        P("ctx", "ch"),
        P("ctx", "ch"),
        P("ch"),
        P("ch", None),
    )
    return jax.shard_map(
        per_device, mesh=mesh, in_specs=in_specs, out_specs=P("ctx", "ch"), check_vma=False
    )
```

```python
import functools

import jax
import jax.numpy as jnp
import numpy as np
from jax import lax
from jax.experimental import pallas as pl
from jax.experimental.pallas import tpu as pltpu
from jax.sharding import PartitionSpec as P

BLOCK = 256
F32 = jnp.float32
BF16 = jnp.bfloat16


def transform_tables(block):
    k = np.arange(block)[:, None]
    n = np.arange(block)[None, :]
    angle = np.pi * (((2 * k + 1) * n) % (4 * block)) / (2 * block)
    forward = np.concatenate([np.cos(angle), -np.sin(angle)], axis=0)
    backward = np.concatenate([np.cos(angle).T, -np.sin(angle).T], axis=1) / block

    def halves(table):
        high = table.astype(BF16)
        low = (table - high.astype(np.float64)).astype(BF16)
        return high, low

    f_high, f_low = halves(forward)
    b_high, b_low = halves(backward)
    return np.stack([f_high, f_low]), np.stack([b_high, b_low])


def dot(left, right):
    return jnp.dot(left, right, preferred_element_type=F32)


MESH = pl.DeviceIdType.MESH


def gate_kernel(n_ctx, q_ref, k_ref, v_ref, h_ref, skip_ref, f_ref, b_ref, w_ref, out_ref, wx,
                outbox, inbox, spec, prod, conv_out, conv_in,
                w_send, w_recv, in_send, in_recv, back_send, back_recv):
    me = lax.axis_index("ctx")
    ch = lax.axis_index("ch")
    core = lax.rem(ch, 2)
    mate = ch + 1 - 2 * core
    n_chip, _, wide = wx.shape
    tokens = q_ref.shape[0]
    width = conv_in.shape[2]
    block = BLOCK
    per = tokens // block
    nb = n_ctx * per

    barrier = pltpu.get_barrier_semaphore()
    pl.semaphore_signal(barrier, inc=1, device_id={"ch": mate}, device_id_type=MESH)
    for d in range(1, n_ctx):
        pl.semaphore_signal(
            barrier, inc=1, device_id={"ctx": lax.rem(me + d, n_ctx)}, device_id_type=MESH
        )

    def rows_of(r):
        return pl.ds(pl.multiple_of(r * block, block), block)

    def fill(r, carry):
        at = rows_of(r)
        for i in range(n_ctx):
            lanes = slice(i * width, (i + 1) * width)
            mixed = k_ref[at, lanes].astype(F32) * v_ref[at, lanes].astype(F32)
            outbox[i, at, :width] = mixed.astype(BF16)
            outbox[i, at, width:] = h_ref[at, lanes]
        return carry

    lax.fori_loop(0, per, fill, 0)
    pl.semaphore_wait(barrier, n_ctx)

    def in_copy(d):
        to = lax.rem(me + d, n_ctx)
        return pltpu.make_async_remote_copy(
            src_ref=outbox.at[to], dst_ref=inbox.at[me],
            send_sem=in_send.at[d], recv_sem=in_recv.at[d],
            device_id={"ctx": to}, device_id_type=MESH,
        )

    def in_wait(d):
        source = lax.rem(me + n_ctx - d, n_ctx)
        pltpu.make_async_remote_copy(
            src_ref=outbox.at[source], dst_ref=inbox.at[source],
            send_sem=in_send.at[d], recv_sem=in_recv.at[d],
            device_id={"ctx": source}, device_id_type=MESH,
        ).wait_recv()

    def back_copy(d):
        to = lax.rem(me + d, n_ctx)
        return pltpu.make_async_remote_copy(
            src_ref=conv_out.at[to], dst_ref=conv_in.at[me],
            send_sem=back_send.at[d], recv_sem=back_recv.at[d],
            device_id={"ctx": to}, device_id_type=MESH,
        )

    def back_wait(d):
        source = lax.rem(me + n_ctx - d, n_ctx)
        pltpu.make_async_remote_copy(
            src_ref=conv_out.at[source], dst_ref=conv_in.at[source],
            send_sem=back_send.at[d], recv_sem=back_recv.at[d],
            device_id={"ctx": source}, device_id_type=MESH,
        ).wait_recv()

    def w_copy(t):
        lanes = pl.ds(pl.multiple_of((t * 2 + 1 - core) * wide, wide), wide)
        return pltpu.make_async_remote_copy(
            src_ref=w_ref.at[:, lanes], dst_ref=wx.at[t],
            send_sem=w_send.at[t], recv_sem=w_recv.at[t],
            device_id={"ch": mate}, device_id_type=MESH,
        )

    for d in range(1, n_ctx):
        in_copy(d).start()
    for t in range(n_chip):
        w_copy(t).start()

    def ahead(box, source):
        def one(r, carry):
            data = box[source, rows_of(r), :]
            spec[source * per + r] = dot(f_ref[0], data) + dot(f_ref[1], data)
            return carry

        lax.fori_loop(0, per, one, 0)

    ahead(outbox, me)
    for d in range(1, n_ctx):
        in_wait(d)
        ahead(inbox, lax.rem(me + n_ctx - d, n_ctx))

    rows = 8
    sign = 1.0 - 2.0 * (lax.broadcasted_iota(jnp.int32, (rows, width), 0) % 2).astype(F32)

    def products(chunk, carry):
        top = pl.multiple_of(chunk * rows, rows)
        re = pl.ds(top, rows)
        im = pl.ds(pl.multiple_of(block + top, rows), rows)
        x = [(spec[p, re, :width], spec[p, im, :width]) for p in range(nb)]
        h = [(spec[p, re, width:], spec[p, im, width:]) for p in range(nb)]
        last = None
        for j in range(nb):
            zr = zi = None
            for p in range(j + 1):
                xr, xi = x[p]
                hr, hi = h[j - p]
                tr = xr * hr - xi * hi
                ti = xr * hi + xi * hr
                zr = tr if zr is None else zr + tr
                zi = ti if zi is None else zi + ti
            if last is None:
                yr, yi = zr, zi
            else:
                yr = zr - sign * last[1]
                yi = zi + sign * last[0]
            last = (zr, zi)
            prod[j, re, :] = yr
            prod[j, im, :] = yi
        return carry

    lax.fori_loop(0, block // rows, products, 0)

    def back(box, to):
        def one(r, carry):
            j = to * per + 2 * r
            data = jnp.concatenate([prod[j], prod[j + 1]], axis=1)
            high = data.astype(BF16)
            low = (data - high.astype(F32)).astype(BF16)
            conv = (dot(b_ref[0], high) + (dot(b_ref[0], low) + dot(b_ref[1], high))).astype(BF16)
            box[to, rows_of(2 * r), :] = conv[:, :width]
            box[to, rows_of(2 * r + 1), :] = conv[:, width:]
            return carry

        lax.fori_loop(0, per // 2, one, 0)

    for d in range(1, n_ctx):
        back(conv_out, lax.rem(me + d, n_ctx))
        back_copy(d).start()
    back(conv_in, me)
    for d in range(1, n_ctx):
        back_wait(d)

    def gate(r, carry):
        at = rows_of(r)
        for i in range(n_ctx):
            lanes = slice(i * width, (i + 1) * width)
            mixed = outbox[i, at, :width].astype(F32)
            total = conv_in[i, at, :].astype(F32) + skip_ref[:, lanes] * mixed
            out_ref[at, lanes] = (q_ref[at, lanes].astype(F32) * total).astype(BF16)
        return carry

    lax.fori_loop(0, per, gate, 0)
    for d in range(1, n_ctx):
        in_copy(d).wait_send()
        back_copy(d).wait_send()
    for t in range(n_chip):
        w_copy(t).wait()


def gated_conv(queries, key_input, value_input, filters, skip_gain, out_weight):
    tokens, channels = queries.shape
    n_ctx = lax.axis_size("ctx")
    n_ch = lax.axis_size("ch")
    n_chip = n_ch // 2
    width = channels // n_ctx
    nb = n_ctx * tokens // BLOCK
    forward, backward = transform_tables(BLOCK)
    vmem = pl.BlockSpec(memory_space=pltpu.VMEM)
    hbm = pl.BlockSpec(memory_space=pl.ANY)
    return pl.pallas_call(
        functools.partial(gate_kernel, n_ctx),
        out_shape=(
            jax.ShapeDtypeStruct((tokens, channels), BF16),
            jax.ShapeDtypeStruct((n_chip, channels, out_weight.shape[1] // n_ch), BF16),
        ),
        in_specs=[vmem] * 7 + [hbm],
        out_specs=(vmem, hbm),
        scratch_shapes=[
            pltpu.VMEM((n_ctx, tokens, 2 * width), BF16),
            pltpu.VMEM((n_ctx, tokens, 2 * width), BF16),
            pltpu.VMEM((nb, 2 * BLOCK, 2 * width), F32),
            pltpu.VMEM((nb, 2 * BLOCK, width), F32),
            pltpu.VMEM((n_ctx, tokens, width), BF16),
            pltpu.VMEM((n_ctx, tokens, width), BF16),
            pltpu.SemaphoreType.DMA((n_chip,)),
            pltpu.SemaphoreType.DMA((n_chip,)),
            pltpu.SemaphoreType.DMA((n_ctx,)),
            pltpu.SemaphoreType.DMA((n_ctx,)),
            pltpu.SemaphoreType.DMA((n_ctx,)),
            pltpu.SemaphoreType.DMA((n_ctx,)),
        ],
        compiler_params=pltpu.CompilerParams(
            collective_id=1, has_side_effects=True, vmem_limit_bytes=56 * 1024 * 1024
        ),
        cost_estimate=pl.CostEstimate(
            flops=28 * n_ctx * tokens * BLOCK * width, bytes_accessed=10 * tokens * channels,
            transcendentals=0,
        ),
    )(queries, key_input, value_input, filters, skip_gain[None, :],
      jnp.asarray(forward), jnp.asarray(backward), out_weight)


CHUNKS = 4


def project_kernel(n_ch, g_ref, w_ref, wx, out_ref, w_own, w_sem, gx, send, from_left, from_right, own,
                   g_send, g_recv, send_sem, left_sem, right_sem):
    me = lax.axis_index("ch")
    chip = lax.div(me, 2)
    core = lax.rem(me, 2)
    mate = chip * 2 + 1 - core
    n_chip = n_ch // 2
    tokens, block = out_ref.shape
    rows = tokens // CHUNKS
    has_left = chip > 0
    has_right = chip < n_chip - 1
    left = jnp.maximum(me - 2, core)
    right = jnp.minimum(me + 2, n_ch - 2 + core)

    def w_load(t):
        lanes = pl.ds(pl.multiple_of((t * 2 + core) * block, block), block)
        return pltpu.make_async_copy(w_ref.at[:, lanes], w_own.at[t], w_sem.at[t])

    for t in range(n_chip):
        w_load(t).start()

    barrier = pltpu.get_barrier_semaphore()
    pl.semaphore_signal(barrier, inc=1, device_id={"ch": mate}, device_id_type=MESH)

    @pl.when(has_left)
    def _():
        pl.semaphore_signal(barrier, inc=1, device_id={"ch": left}, device_id_type=MESH)

    @pl.when(has_right)
    def _():
        pl.semaphore_signal(barrier, inc=1, device_id={"ch": right}, device_id_type=MESH)

    pl.semaphore_wait(barrier, 1 + has_left.astype(jnp.int32) + has_right.astype(jnp.int32))

    def columns(chip_at, core_at):
        return pl.ds(pl.multiple_of((chip_at * 2 + core_at) * block, block), block)

    def tokens_of(m):
        return pl.ds(pl.multiple_of(m * rows, rows), rows)

    def remote(src, dst, sent, arrived, target):
        return pltpu.make_async_remote_copy(
            src_ref=src, dst_ref=dst, send_sem=sent, recv_sem=arrived,
            device_id={"ch": target}, device_id_type=MESH,
        )

    def g_copy(m):
        at = tokens_of(m)
        return remote(g_ref.at[at], gx.at[at], g_send.at[m], g_recv.at[m], mate)

    def to_right(t, m):
        at = tokens_of(m)
        return remote(send.at[t, at], from_left.at[t, at], send_sem.at[t, m], left_sem.at[t, m], right)

    def to_left(t, m):
        at = tokens_of(m)
        return remote(send.at[t, at], from_right.at[t, at], send_sem.at[t, m], right_sem.at[t, m], left)

    def arrive_left(t, m):
        at = tokens_of(m)
        return remote(send.at[t, at], from_left.at[t, at], send_sem.at[t, m], left_sem.at[t, m], left)

    def arrive_right(t, m):
        at = tokens_of(m)
        return remote(send.at[t, at], from_right.at[t, at], send_sem.at[t, m], right_sem.at[t, m], right)

    for m in range(CHUNKS):
        g_copy(m).start()

    for t in range(n_chip):
        w_load(t).wait()

    def share(t, m):
        at = tokens_of(m)
        return dot(g_ref[at, :], w_own[t]) + dot(gx[at, :], wx[t])

    def pass_on(t, m, first, arrived, copy):
        at = tokens_of(m)
        part = share(t, m)

        @pl.when(first)
        def _():
            send[t, at, :] = part.astype(BF16)

        @pl.when(jnp.logical_not(first))
        def _():
            arrived(t, m)

        @pl.when(jnp.logical_not(first))
        def _():
            buffer = from_left if copy is to_right else from_right
            send[t, at, :] = (part + buffer[t, at, :].astype(F32)).astype(BF16)

        copy(t, m).start()

    def drain(m):
        for d in range(n_chip - 1, 0, -1):
            @pl.when(chip + d < n_chip)
            def _():
                to_right(chip + d, m).wait_send()

            @pl.when(chip - d >= 0)
            def _():
                to_left(chip - d, m).wait_send()

    def step(m, carry):
        g_copy(m).wait()

        @pl.when(m >= 2)
        def _():
            drain(m - 2)

        for d in range(n_chip - 1, 0, -1):
            @pl.when(chip + d < n_chip)
            def _():
                pass_on(chip + d, m, jnp.logical_not(has_left),
                        lambda t, m: arrive_left(t, m).wait_recv(), to_right)

            @pl.when(chip - d >= 0)
            def _():
                pass_on(chip - d, m, jnp.logical_not(has_right),
                        lambda t, m: arrive_right(t, m).wait_recv(), to_left)

        own[tokens_of(m), :] = share(chip, m)
        return carry

    lax.fori_loop(0, CHUNKS, step, 0)

    def finish(m, carry):
        at = tokens_of(m)

        @pl.when(has_left)
        def _():
            arrive_left(chip, m).wait_recv()
            own[at, :] += from_left[chip, at, :].astype(F32)

        @pl.when(has_right)
        def _():
            arrive_right(chip, m).wait_recv()
            own[at, :] += from_right[chip, at, :].astype(F32)

        out_ref[at, :] = own[at, :].astype(BF16)
        return carry

    lax.fori_loop(0, CHUNKS, finish, 0)
    drain(CHUNKS - 2)
    drain(CHUNKS - 1)


def project(gated, out_weight, mate_weight):
    tokens, channels = gated.shape
    n_ch = lax.axis_size("ch")
    n_chip = n_ch // 2
    block = out_weight.shape[1] // n_ch
    return pl.pallas_call(
        functools.partial(project_kernel, n_ch),
        out_shape=jax.ShapeDtypeStruct((tokens, block), BF16),
        in_specs=[
            pl.BlockSpec(memory_space=pltpu.VMEM),
            pl.BlockSpec(memory_space=pl.ANY),
            pl.BlockSpec(memory_space=pltpu.VMEM),
        ],
        out_specs=pl.BlockSpec(memory_space=pltpu.VMEM),
        scratch_shapes=[
            pltpu.VMEM((n_chip, channels, block), BF16),
            pltpu.SemaphoreType.DMA((n_chip,)),
            pltpu.VMEM((tokens, channels), BF16),
            pltpu.VMEM((n_chip, tokens, block), BF16),
            pltpu.VMEM((n_chip, tokens, block), BF16),
            pltpu.VMEM((n_chip, tokens, block), BF16),
            pltpu.VMEM((tokens, block), F32),
            pltpu.SemaphoreType.DMA((CHUNKS,)),
            pltpu.SemaphoreType.DMA((CHUNKS,)),
            pltpu.SemaphoreType.DMA((n_chip, CHUNKS)),
            pltpu.SemaphoreType.DMA((n_chip, CHUNKS)),
            pltpu.SemaphoreType.DMA((n_chip, CHUNKS)),
        ],
        compiler_params=pltpu.CompilerParams(
            collective_id=0, has_side_effects=True, vmem_limit_bytes=48 * 1024 * 1024
        ),
        cost_estimate=pl.CostEstimate(
            flops=2 * tokens * channels * n_ch * block,
            bytes_accessed=2 * channels * n_ch * block, transcendentals=0,
        ),
    )(gated, out_weight, mate_weight)


def per_device(queries, key_input, value_input, filters, skip_gain, out_weight):
    gated, mate_weight = gated_conv(
        queries, key_input, value_input, filters, skip_gain, out_weight
    )
    return project(gated, out_weight, mate_weight)


def solution(mesh):
    in_specs = (
        P("ctx", "ch"),
        P("ctx", "ch"),
        P("ctx", "ch"),
        P("ctx", "ch"),
        P("ch"),
        P("ch", None),
    )
    return jax.shard_map(
        per_device, mesh=mesh, in_specs=in_specs, out_specs=P("ctx", "ch"), check_vma=False
    )
```
